32 devices in a mesh: seq: 8 (over z, x), head: 4 (over y, core).
Axes of the slice: x: 2, y: 2, z: 4, core: 2. Of those that a mesh axis runs over, the one named last changes fastest.
Arguments:
- q_in: bfloat16 [16384, 2048], P(('seq', 'head')), may hold values from -6 to 6
- k_in: bfloat16 [16384, 2048], P(('seq', 'head')), may hold values from -6 to 6
- v_in: bfloat16 [16384, 2048], P(('seq', 'head')), may hold values from -6 to 6
- beta: bfloat16 [16384, 16], P(('seq', 'head')), may hold values from 0 to 1, as said below
- conv_q: float32 [4, 2048], replicated, may hold values from -3 to 3
- conv_k: float32 [4, 2048], replicated, may hold values from -3 to 3
- conv_v: float32 [4, 2048], replicated, may hold values from -3 to 3
- out_gain: float32 [128], replicated, may hold values from 0.25 to 1.75
Outputs:
- mixed: bfloat16 [16384, 2048], P(('seq', 'head'))
The draws below stay inside these ranges and needn't reach their ends.
Inputs may be any that keep to these rules, and one draw needn't show every extreme that they name: `beta`: write strengths of the delta rule, positive.
All inputs are finite; a program needn't handle non-finite values.
Results may differ from the reference program's by a relative error of at most 0.001.
Values may be sent and summed in bfloat16 or wider, within the bound.
A program may use at most 576 MiB of HBM per device.

```python
import math
import jax
import jax.numpy as jnp
from jax import lax

HEAD_NUMBER = 16
KEY_WIDTH = 128
DV = 128
BLOCK = 64
KW = 4
TRACE_TOKENS = 16384


def draw_beta(key, part):
    key_order = jax.random.fold_in(key, 11)
    key_slow = jax.random.fold_in(key, 12)
    key_fast = jax.random.fold_in(key, 13)
    key_jitter = jax.random.fold_in(key, 14)
    surge_seed = jax.random.fold_in(key, 15)
    level_seed = jax.random.fold_in(key, 16)
    plateau_seed = jax.random.fold_in(key, 17)
    plateau_level_seed = jax.random.fold_in(key, 18)
    rank_order = jax.random.permutation(key_order, HEAD_NUMBER)
    sluggish_heads = rank_order < HEAD_NUMBER // 2
    slow_rate = jax.random.uniform(key_slow, (HEAD_NUMBER,), jnp.float32, 0.2, 1.0) * (KEY_WIDTH / TRACE_TOKENS)
    fast_rate = jnp.exp(jax.random.uniform(key_fast, (HEAD_NUMBER,), jnp.float32, math.log(0.1), math.log(0.9)))
    head_rate = jnp.where(sluggish_heads, slow_rate, fast_rate)
    jitter = jax.random.uniform(key_jitter, (TRACE_TOKENS, HEAD_NUMBER), jnp.float32, 0.5, 1.5)
    surge_strength = head_rate[None, :] * jitter
    token_places = jnp.arange(TRACE_TOKENS)
    plateau_span = 4 * BLOCK
    slot_count = TRACE_TOKENS // plateau_span
    plateau_count = max(TRACE_TOKENS // (64 * BLOCK), 1)
    chosen_slots = jax.random.permutation(plateau_seed, slot_count)[:plateau_count]
    token_slot = token_places // plateau_span
    within_plateau = jnp.any(token_slot[:, None] == chosen_slots[None, :], axis=1)
    plateau_height = jax.random.uniform(plateau_level_seed, (TRACE_TOKENS, HEAD_NUMBER), jnp.float32, 0.016, 0.0196)
    surge_strength = jnp.where(within_plateau[:, None] & sluggish_heads[None, :], plateau_height, surge_strength)
    surge_length = max(KEY_WIDTH // 4, 2)
    surge_onset = jax.random.randint(surge_seed, (4,), 0, TRACE_TOKENS - surge_length)
    within_surge = jnp.any((token_places[:, None] >= surge_onset[None, :]) & (token_places[:, None] < surge_onset[None, :] + surge_length), axis=1)
    surge_height = jax.random.uniform(level_seed, (TRACE_TOKENS, HEAD_NUMBER), jnp.float32, 0.5, 1.0)
    surge_strength = jnp.where(within_surge[:, None] & sluggish_heads[None, :], surge_height, surge_strength)
    return jnp.minimum(surge_strength, 1.0).astype(jnp.bfloat16)


def block_scale(key, shape, cuts, least, largest):
    level = 1.0
    for position, blocks in cuts:
        draws = jax.random.uniform(jax.random.fold_in(jax.random.fold_in(key, 6), position), (blocks,), jnp.float32, least / len(cuts), largest / len(cuts))
        level = level * jnp.repeat(jnp.exp(draws), shape[position] // blocks).reshape((-1,) + (1,) * (len(shape) - 1 - position))
    return level


def bell_draw(rng, shape, spread, bound, shards=(), held_as=jnp.bfloat16):
    level = block_scale(rng, shape, shards, -0.22, 0.18) if shards else 1.0
    result = jax.random.normal(rng, shape, jnp.float32) * spread * level
    return jnp.minimum(jnp.maximum(result, -bound), bound).astype(held_as)


def setup_inputs(seed: int = 0) -> dict:
    keys = jax.random.split(jax.random.key(seed), 9)
    return {
        "q_in": bell_draw(keys[0], (TRACE_TOKENS, HEAD_NUMBER * KEY_WIDTH), 1.0, 6.0, ((0, 32),)),
        "k_in": bell_draw(keys[1], (TRACE_TOKENS, HEAD_NUMBER * KEY_WIDTH), 1.0, 6.0, ((0, 32),)),
        "v_in": bell_draw(keys[2], (TRACE_TOKENS, HEAD_NUMBER * DV), 1.0, 6.0, ((0, 32),)),
        "beta": draw_beta(jax.random.fold_in(keys[8], 71), 0),
        "conv_q": bell_draw(keys[4], (KW, HEAD_NUMBER * KEY_WIDTH), KW ** -0.5, 3.0, (), jnp.float32),
        "conv_k": bell_draw(keys[5], (KW, HEAD_NUMBER * KEY_WIDTH), KW ** -0.5, 3.0, (), jnp.float32),
        "conv_v": bell_draw(keys[6], (KW, HEAD_NUMBER * DV), KW ** -0.5, 3.0, (), jnp.float32),
        "out_gain": jnp.clip(1.0 + 0.15 * jax.random.normal(keys[7], (DV,), jnp.float32), 0.25, 1.75),
    }


peak_level = lax.Precision.HIGHEST

def causal_conv(padded, weight, length):
    summed = weight[0] * padded[0:length]
    for offset in range(1, weight.shape[0]):
        summed = summed + weight[offset] * padded[offset:offset + length]
    return summed

def unit_rows(vectors):
    return vectors / jnp.sqrt(lax.optimization_barrier(jnp.sum(vectors * vectors, axis=-1, keepdims=True)) + 1e-06)

def features(q_pad, k_pad, v_pad, beta_rows, conv_q, conv_k, conv_v):
    length = beta_rows.shape[0]
    head_count = beta_rows.shape[1]
    q_conv = causal_conv(q_pad.astype(jnp.float32), conv_q, length)
    k_conv = causal_conv(k_pad.astype(jnp.float32), conv_k, length)
    v_conv = causal_conv(v_pad.astype(jnp.float32), conv_v, length)
    queries = unit_rows(jax.nn.silu(q_conv).reshape(length, head_count, -1))
    key_rows = unit_rows(jax.nn.silu(k_conv).reshape(length, head_count, -1))
    values = jax.nn.silu(v_conv).reshape(length, head_count, -1)
    return (queries, key_rows, values, beta_rows.astype(jnp.float32))

def block_parts(queries, key_rows, values, surge_strength):
    length, head_count, ignored = key_rows.shape
    block_count = length // BLOCK

    def to_blocks(matrix):
        return jnp.swapaxes(matrix.reshape(block_count, BLOCK, head_count, matrix.shape[-1]), 1, 2)
    query_tiles = to_blocks(queries)
    key_tiles = to_blocks(key_rows)
    v_blocks = to_blocks(values)
    s_blocks = jnp.swapaxes(surge_strength.reshape(block_count, BLOCK, head_count), 1, 2)[..., None]
    scaled_k = key_tiles * s_blocks
    gram_rows = jnp.einsum('nhik,nhjk->nhij', scaled_k, key_tiles, precision=peak_level)
    system = jnp.tril(gram_rows, -1) + jnp.eye(BLOCK, dtype=gram_rows.dtype)
    weight_rows = lax.linalg.triangular_solve(system, scaled_k, left_side=True, lower=True, unit_diagonal=True)
    update_rows = lax.linalg.triangular_solve(system, v_blocks * s_blocks, left_side=True, lower=True, unit_diagonal=True)
    attention_scores = jnp.tril(jnp.einsum('nhik,nhjk->nhij', query_tiles, key_tiles, precision=peak_level))
    return (query_tiles, key_tiles, weight_rows, update_rows, attention_scores)

def run_blocks(carried, parts):

    def advance(present_value, pieces):
        query_tiles, key_tiles, weight_rows, update_rows, attention_scores = pieces
        fresh_values = update_rows - jnp.einsum('jel,jlm->jem', weight_rows, present_value, precision=peak_level)
        blended_rows = jnp.einsum('jel,jlm->jem', query_tiles, present_value, precision=peak_level) + jnp.einsum('ezq,eqd->ezd', attention_scores, fresh_values, precision=peak_level)
        present_value = present_value + jnp.einsum('pty,ptn->pyn', key_tiles, fresh_values, precision=peak_level)
        return (present_value, blended_rows)
    ignored, outputs = lax.scan(advance, carried, parts)
    block_count, head_count, rows_block, width = outputs.shape
    return jnp.swapaxes(outputs, 1, 2).reshape(block_count * rows_block, head_count, width)

def finish(outputs, out_gain):
    inv_rms = lax.rsqrt(lax.optimization_barrier(jnp.mean(outputs * outputs, axis=-1, keepdims=True)) + 1e-05)
    return (outputs * inv_rms * out_gain).reshape(outputs.shape[0], -1).astype(jnp.bfloat16)

def reference(q_in, k_in, v_in, beta, conv_q, conv_k, conv_v, out_gain):
    pad_rows = jnp.zeros((KW - 1, q_in.shape[1]), q_in.dtype)
    pad_vals = jnp.zeros((KW - 1, v_in.shape[1]), v_in.dtype)
    q_pad = jnp.concatenate([pad_rows, q_in], axis=0)
    k_pad = jnp.concatenate([pad_rows, k_in], axis=0)
    v_pad = jnp.concatenate([pad_vals, v_in], axis=0)
    queries, key_rows, values, surge_strength = features(q_pad, k_pad, v_pad, beta, conv_q, conv_k, conv_v)
    parts = block_parts(queries, key_rows, values, surge_strength)
    carried = jnp.zeros((HEAD_NUMBER, KEY_WIDTH, DV), jnp.float32)
    return finish(run_blocks(carried, parts), out_gain)
```

```python
import functools
import jax
import jax.numpy as jnp
from jax import lax
from jax.experimental import pallas as pl
from jax.experimental.pallas import tpu as pltpu
from jax.sharding import PartitionSpec as P

WIDTH = 128
CHUNK = 128
KW = 4
RIM = 16
BASE = 8
HEADS_PER_STEP = 2

F32 = jnp.float32
BF16 = jnp.bfloat16
peak_level = lax.Precision.HIGHEST


def split(x):
    hi = x.astype(BF16)
    return hi, (x - hi.astype(F32)).astype(BF16)


def dot(a, b):
    return jnp.dot(a, b, preferred_element_type=F32)


def wide_left(a):
    hi, lo = split(a)
    return jnp.concatenate([hi, lo], axis=1)


def square_right(b):
    row = jnp.concatenate(split(b), axis=1)
    return jnp.concatenate([row, row], axis=0)


def fold(x):
    return x[:, :WIDTH] + x[:, WIDTH:]


def mm_square(a, b):
    return fold(dot(wide_left(a), square_right(b)))


def mm_wide(a, b):
    hi, lo = split(b)
    left = wide_left(a)
    return dot(left, jnp.concatenate([hi, hi], axis=0)) + dot(left[:, : a.shape[1]], lo)


def gram(rows, keys):
    hi, lo = split(keys)
    right = jnp.concatenate(
        [jnp.concatenate([hi, hi], axis=1), jnp.concatenate([lo, lo], axis=1)], axis=0
    )
    out = lax.dot_general(
        wide_left(rows), right, (((1,), (1,)), ((), ())), preferred_element_type=F32
    )
    return fold(out)


def lower_inverse(g):
    lane = lax.broadcasted_iota(jnp.int32, (BASE, CHUNK), 1)
    sub = lax.broadcasted_iota(jnp.int32, (BASE, CHUNK), 0)
    groups = CHUNK // BASE
    packed = jnp.zeros((BASE, CHUNK), F32)
    for i in range(groups):
        packed = jnp.where(lane // BASE == i, g[i * BASE : (i + 1) * BASE, :], packed)
    x = jnp.where(lane % BASE == sub, 1.0, 0.0).astype(F32)
    for j in range(BASE - 1):
        column = jnp.where(lane % BASE == j, packed, 0.0)
        if j:
            column = pltpu.roll(column, CHUNK - j, 1)
        for by in (1, 2, 4):
            column = column + pltpu.roll(column, by, 1)
        x = x - column * jnp.broadcast_to(x[j : j + 1, :], (BASE, CHUNK))
    inv = jnp.concatenate(
        [jnp.where(lane // BASE == i, x, 0.0) for i in range(groups)], axis=0
    )
    col = lax.broadcasted_iota(jnp.int32, (CHUNK, CHUNK), 1)
    row = lax.broadcasted_iota(jnp.int32, (CHUNK, CHUNK), 0)
    size = BASE
    while size < CHUNK:
        pairs = CHUNK // (2 * size)
        low = [slice((2 * p + 1) * size, (2 * p + 2) * size) for p in range(pairs)]
        up = [slice(2 * p * size, (2 * p + 1) * size) for p in range(pairs)]
        corner = jnp.where(col // size == row // size - 1, g, 0.0)
        corner = jnp.concatenate([corner[s] for s in low], axis=0)
        old = jnp.concatenate([inv[s] for s in low], axis=0)
        e = mm_square(corner, inv)
        zero = jnp.zeros((size, CHUNK), F32)
        e_full = jnp.concatenate(
            [t for p in range(pairs) for t in (zero, e[p * size : (p + 1) * size])], axis=0
        )
        new = old - mm_square(old, e_full)
        inv = jnp.concatenate(
            [t for p in range(pairs) for t in (inv[up[p]], new[p * size : (p + 1) * size])],
            axis=0,
        )
        size *= 2
    return inv


def conv_silu(x_ref, rim_ref, w_ref, pad, lanes):
    length = x_ref.shape[0]
    pad[0:RIM, :] = rim_ref[:, lanes].astype(F32)
    pad[RIM : RIM + length, :] = x_ref[:, lanes].astype(F32)
    w = w_ref[:, lanes]
    first = RIM - (KW - 1)
    summed = w[0:1, :] * pad[first : first + length, :]
    for j in range(1, KW):
        summed = summed + w[j : j + 1, :] * pad[first + j : first + j + length, :]
    return summed / (1.0 + jnp.exp(-summed))


def unit_rows(x):
    return x * lax.rsqrt(jnp.sum(x * x, axis=-1, keepdims=True) + 1e-06)


def local_kernel(q_ref, k_ref, v_ref, b_ref, qr_ref, kr_ref, vr_ref, cq_ref, ck_ref, cv_ref,
                 out_ref, sum_ref, *pads):
    length = q_ref.shape[0]
    step = pl.program_id(0)
    chunks = length // CHUNK
    row = lax.broadcasted_iota(jnp.int32, (CHUNK, CHUNK), 0)
    col = lax.broadcasted_iota(jnp.int32, (CHUNK, CHUNK), 1)
    beta = b_ref[...]
    which = lax.broadcasted_iota(jnp.int32, beta.shape, 1)
    prepared = []
    for i in range(HEADS_PER_STEP):
        lanes = slice(i * WIDTH, (i + 1) * WIDTH)
        q = unit_rows(conv_silu(q_ref, qr_ref, cq_ref, pads[3 * i], lanes))
        k = unit_rows(conv_silu(k_ref, kr_ref, ck_ref, pads[3 * i + 1], lanes))
        v = conv_silu(v_ref, vr_ref, cv_ref, pads[3 * i + 2], lanes)
        head = step * HEADS_PER_STEP + i
        b = jnp.sum(jnp.where(which == head, beta, 0.0), axis=1, keepdims=True)
        parts = []
        for n in range(chunks):
            rows = slice(n * CHUNK, (n + 1) * CHUNK)
            qn, kn, vn, bn = q[rows], k[rows], v[rows], b[rows]
            both = gram(jnp.concatenate([qn, kn], axis=0), kn)
            p = jnp.where(row >= col, both[:CHUNK], 0.0)
            g = jnp.where(row > col, both[CHUNK:] * bn, 0.0)
            inv = lower_inverse(g)
            wu = mm_wide(inv, jnp.concatenate([kn * bn, vn * bn], axis=1))
            parts.append((qn, jnp.concatenate([p, kn.T], axis=0), wu))
        prepared.append(parts)
    zero = jnp.zeros((CHUNK, WIDTH), F32)
    carried = [None] * HEADS_PER_STEP
    for n in range(chunks):
        for i in range(HEADS_PER_STEP):
            qn, pk, wu = prepared[i][n]
            w, u = wu[:, :WIDTH], wu[:, WIDTH:]
            if n == 0:
                fresh = jnp.concatenate([-w, u], axis=1)
                seen = jnp.concatenate([qn, zero], axis=1)
                eye = jnp.where(row == col, 1.0, 0.0).astype(F32)
                state = jnp.concatenate([eye, zero], axis=1)
            else:
                state = carried[i]
                moved = mm_wide(jnp.concatenate([w, qn], axis=0), state)
                fresh = jnp.concatenate([zero, u], axis=1) - moved[:CHUNK]
                seen = moved[CHUNK:]
            added = mm_wide(pk, fresh)
            out_ref[i, n * CHUNK : (n + 1) * CHUNK, :] = seen + added[:CHUNK]
            carried[i] = state + added[CHUNK:]
    for i in range(HEADS_PER_STEP):
        sum_ref[i, :, :] = carried[i]


def local_pass(q, k, v, beta, rims, conv_q, conv_k, conv_v):
    length, total = q.shape
    heads = total // WIDTH
    wide = HEADS_PER_STEP * WIDTH
    rows = pl.BlockSpec((length, wide), lambda h: (0, h))
    rim = pl.BlockSpec((RIM, wide), lambda h: (0, h))
    taps = pl.BlockSpec((KW, wide), lambda h: (0, h))
    return pl.pallas_call(
        local_kernel,
        grid=(heads // HEADS_PER_STEP,),
        in_specs=[rows, rows, rows, pl.BlockSpec((length, heads), lambda h: (0, 0)),
                  rim, rim, rim, taps, taps, taps],
        out_specs=[
            pl.BlockSpec((HEADS_PER_STEP, length, 2 * WIDTH), lambda h: (h, 0, 0)),
            pl.BlockSpec((HEADS_PER_STEP, WIDTH, 2 * WIDTH), lambda h: (h, 0, 0)),
        ],
        out_shape=[
            jax.ShapeDtypeStruct((heads, length, 2 * WIDTH), F32),
            jax.ShapeDtypeStruct((heads, WIDTH, 2 * WIDTH), F32),
        ],
        scratch_shapes=[pltpu.VMEM((RIM + length, WIDTH), F32)] * (3 * HEADS_PER_STEP),
        compiler_params=pltpu.CompilerParams(vmem_limit_bytes=48 * 2**20),
        name="local_pass",
    )(q, k, v, beta, *rims, conv_q, conv_k, conv_v)


def finish_kernel(part_ref, state_ref, gain_ref, out_ref):
    for i in range(part_ref.shape[0]):
        part = part_ref[i]
        o = part[:, WIDTH:] + mm_square(part[:, :WIDTH], state_ref[i])
        scale = lax.rsqrt(jnp.mean(o * o, axis=-1, keepdims=True) + 1e-05)
        out_ref[:, i * WIDTH : (i + 1) * WIDTH] = (o * scale * gain_ref[...]).astype(BF16)


def finish_pass(parts, states, gain):
    heads, length, ignored = parts.shape
    per = 2
    return pl.pallas_call(
        finish_kernel,
        grid=(heads // per,),
        in_specs=[
            pl.BlockSpec((per, length, 2 * WIDTH), lambda h: (h, 0, 0)),
            pl.BlockSpec((per, WIDTH, WIDTH), lambda h: (h, 0, 0)),
            pl.BlockSpec((1, WIDTH), lambda h: (0, 0)),
        ],
        out_specs=pl.BlockSpec((length, per * WIDTH), lambda h: (0, h)),
        out_shape=jax.ShapeDtypeStruct((length, heads * WIDTH), BF16),
        compiler_params=pltpu.CompilerParams(vmem_limit_bytes=48 * 2**20),
        name="finish_pass",
    )(parts, states, gain.reshape(1, WIDTH))


def shifted(value, axis):
    peers = lax.axis_size(axis)
    return lax.ppermute(value, axis, [(i, i + 1) for i in range(peers - 1)])


def times(a, b):
    return jnp.einsum("hij,hjv->hiv", a, b, precision=peak_level)


def incoming_states(summary):
    group = lax.axis_size("head")
    held = lax.all_to_all(summary, "head", split_axis=0, concat_axis=0, tiled=True)
    held = held.reshape(group, -1, WIDTH, 2 * WIDTH)
    before = [None, held[0]]
    for c in range(1, group):
        moved = times(held[c][:, :, :WIDTH], before[-1])
        before.append(moved.at[:, :, WIDTH:].add(held[c][:, :, WIDTH:]))
    transfer, local = before[-1][:, :, :WIDTH], before[-1][:, :, WIDTH:]
    arrived = jnp.zeros_like(local)
    for ignored in range(lax.axis_size("seq") - 1):
        arrived = shifted(times(transfer, arrived) + local, "seq")
    states = [arrived]
    for c in range(1, group):
        states.append(times(before[c][:, :, :WIDTH], arrived) + before[c][:, :, WIDTH:])
    states = jnp.concatenate(states, axis=0)
    return lax.all_to_all(states, "head", split_axis=0, concat_axis=0, tiled=True)


def shards(q_in, k_in, v_in, beta, conv_q, conv_k, conv_v, out_gain):
    edges = jnp.stack([q_in[-RIM:], k_in[-RIM:], v_in[-RIM:]])
    rims = shifted(edges, ("seq", "head"))
    parts, summary = local_pass(
        q_in, k_in, v_in, beta.astype(F32), [rims[0], rims[1], rims[2]], conv_q, conv_k, conv_v
    )
    return finish_pass(parts, incoming_states(summary), out_gain)


def solution(mesh):
    rows = P(("seq", "head"), None)
    in_specs = (rows, rows, rows, rows, P(), P(), P(), P())
    return jax.shard_map(
        shards, mesh=mesh, in_specs=in_specs, out_specs=rows, check_vma=False
    )
```

```python
import functools
import jax
import jax.numpy as jnp
from jax import lax
from jax.experimental import pallas as pl
from jax.experimental.pallas import tpu as pltpu
from jax.sharding import PartitionSpec as P

WIDTH = 128
CHUNK = 128
KW = 4
RIM = 16
BASE = 8
HEADS_PER_STEP = 4

F32 = jnp.float32
BF16 = jnp.bfloat16
peak_level = lax.Precision.HIGHEST


def split(x):
    hi = x.astype(BF16)
    return hi, (x - hi.astype(F32)).astype(BF16)


def dot(a, b):
    return jnp.dot(a, b, preferred_element_type=F32)


def wide_left(a):
    hi, lo = split(a)
    return jnp.concatenate([hi, lo], axis=1)


def square_right(b):
    row = jnp.concatenate(split(b), axis=1)
    return jnp.concatenate([row, row], axis=0)


def fold(x):
    return x[:, :WIDTH] + x[:, WIDTH:]


def mm_square(a, b):
    return fold(dot(wide_left(a), square_right(b)))


def mm_wide(a, b):
    hi, lo = split(b)
    left = wide_left(a)
    return dot(left, jnp.concatenate([hi, hi], axis=0)) + dot(left[:, : a.shape[1]], lo)


def gram(rows, keys):
    hi, lo = split(keys)
    right = jnp.concatenate(
        [jnp.concatenate([hi, hi], axis=1), jnp.concatenate([lo, lo], axis=1)], axis=0
    )
    out = lax.dot_general(
        wide_left(rows), right, (((1,), (1,)), ((), ())), preferred_element_type=F32
    )
    return fold(out)


def base_inverse(g):
    lane = lax.broadcasted_iota(jnp.int32, (BASE, CHUNK), 1)
    sub = lax.broadcasted_iota(jnp.int32, (BASE, CHUNK), 0)
    groups = CHUNK // BASE
    packed = jnp.zeros((BASE, CHUNK), F32)
    for i in range(groups):
        packed = jnp.where(lane // BASE == i, g[i * BASE : (i + 1) * BASE, :], packed)
    x = jnp.where(lane % BASE == sub, 1.0, 0.0).astype(F32)
    for j in range(BASE - 1):
        column = jnp.where(lane % BASE == j, packed, 0.0)
        if j:
            column = pltpu.roll(column, CHUNK - j, 1)
        for by in (1, 2, 4):
            column = column + pltpu.roll(column, by, 1)
        x = x - column * jnp.broadcast_to(x[j : j + 1, :], (BASE, CHUNK))
    return jnp.concatenate(
        [jnp.where(lane // BASE == i, x, 0.0) for i in range(groups)], axis=0
    )


def lower_inverses(gs):
    invs = [base_inverse(g) for g in gs]
    col = lax.broadcasted_iota(jnp.int32, (CHUNK, CHUNK), 1)
    row = lax.broadcasted_iota(jnp.int32, (CHUNK, CHUNK), 0)
    size = BASE
    while size < CHUNK:
        pairs = CHUNK // (2 * size)
        low = [slice((2 * p + 1) * size, (2 * p + 2) * size) for p in range(pairs)]
        up = [slice(2 * p * size, (2 * p + 1) * size) for p in range(pairs)]
        corner_mask = col // size == row // size - 1
        zero = jnp.zeros((size, CHUNK), F32)
        olds, products = [], []
        for g, inv in zip(gs, invs):
            corner = jnp.where(corner_mask, g, 0.0)
            corner = jnp.concatenate([corner[s] for s in low], axis=0)
            olds.append(jnp.concatenate([inv[s] for s in low], axis=0))
            products.append(mm_square(corner, inv))
        fulls = [
            jnp.concatenate(
                [t for p in range(pairs) for t in (zero, e[p * size : (p + 1) * size])], axis=0
            )
            for e in products
        ]
        news = [old - mm_square(old, full) for old, full in zip(olds, fulls)]
        invs = [
            jnp.concatenate(
                [t for p in range(pairs) for t in (inv[up[p]], new[p * size : (p + 1) * size])],
                axis=0,
            )
            for inv, new in zip(invs, news)
        ]
        size *= 2
    return invs


def conv_silu(x_ref, rim_ref, w_ref, pad, lanes):
    length = x_ref.shape[0]
    pad[0:RIM, :] = rim_ref[:, lanes].astype(F32)
    pad[RIM : RIM + length, :] = x_ref[:, lanes].astype(F32)
    w = w_ref[:, lanes]
    first = RIM - (KW - 1)
    summed = w[0:1, :] * pad[first : first + length, :]
    for j in range(1, KW):
        summed = summed + w[j : j + 1, :] * pad[first + j : first + j + length, :]
    return summed / (1.0 + jnp.exp(-summed))


def unit_rows(x):
    return x * lax.rsqrt(jnp.sum(x * x, axis=-1, keepdims=True) + 1e-06)


def local_kernel(q_ref, k_ref, v_ref, b_ref, qr_ref, kr_ref, vr_ref, cq_ref, ck_ref, cv_ref,
                 out_ref, sum_ref, *pads):
    length = q_ref.shape[0]
    step = pl.program_id(0)
    chunks = length // CHUNK
    row = lax.broadcasted_iota(jnp.int32, (CHUNK, CHUNK), 0)
    col = lax.broadcasted_iota(jnp.int32, (CHUNK, CHUNK), 1)
    beta = b_ref[...]
    which = lax.broadcasted_iota(jnp.int32, beta.shape, 1)
    chunk_rows, grams, scores = [], [], []
    for i in range(HEADS_PER_STEP):
        lanes = slice(i * WIDTH, (i + 1) * WIDTH)
        q = unit_rows(conv_silu(q_ref, qr_ref, cq_ref, pads[3 * i], lanes))
        k = unit_rows(conv_silu(k_ref, kr_ref, ck_ref, pads[3 * i + 1], lanes))
        v = conv_silu(v_ref, vr_ref, cv_ref, pads[3 * i + 2], lanes)
        head = step * HEADS_PER_STEP + i
        b = jnp.sum(jnp.where(which == head, beta, 0.0), axis=1, keepdims=True)
        for n in range(chunks):
            rows = slice(n * CHUNK, (n + 1) * CHUNK)
            qn, kn, vn, bn = q[rows], k[rows], v[rows], b[rows]
            both = gram(jnp.concatenate([qn, kn], axis=0), kn)
            p = jnp.where(row >= col, both[:CHUNK], 0.0)
            grams.append(jnp.where(row > col, both[CHUNK:] * bn, 0.0))
            scores.append(jnp.concatenate([p, kn.T], axis=0))
            chunk_rows.append((qn, jnp.concatenate([kn * bn, vn * bn], axis=1)))
    prepared = [
        (qn, pk, mm_wide(inv, kv))
        for (qn, kv), pk, inv in zip(chunk_rows, scores, lower_inverses(grams))
    ]
    zero = jnp.zeros((CHUNK, WIDTH), F32)
    for n in range(chunks):
        now = [prepared[i * chunks + n] for i in range(HEADS_PER_STEP)]
        if n == 0:
            eye = jnp.where(row == col, 1.0, 0.0).astype(F32)
            states = [jnp.concatenate([eye, zero], axis=1)] * HEADS_PER_STEP
            fresh = [
                jnp.concatenate([-wu[:, :WIDTH], wu[:, WIDTH:]], axis=1) for ignored, pk, wu in now
            ]
            seen = [jnp.concatenate([qn, zero], axis=1) for qn, pk, wu in now]
        else:
            moved = [
                mm_wide(jnp.concatenate([wu[:, :WIDTH], qn], axis=0), state)
                for (qn, pk, wu), state in zip(now, states)
            ]
            fresh = [
                jnp.concatenate([zero, wu[:, WIDTH:]], axis=1) - m[:CHUNK]
                for (qn, pk, wu), m in zip(now, moved)
            ]
            seen = [m[CHUNK:] for m in moved]
        added = [mm_wide(pk, f) for (qn, pk, wu), f in zip(now, fresh)]
        for i in range(HEADS_PER_STEP):
            out_ref[i, n * CHUNK : (n + 1) * CHUNK, :] = seen[i] + added[i][:CHUNK]
        states = [state + a[CHUNK:] for state, a in zip(states, added)]
    for i in range(HEADS_PER_STEP):
        sum_ref[i, :, :] = states[i]


def local_pass(q, k, v, beta, rims, conv_q, conv_k, conv_v):
    length, total = q.shape
    heads = total // WIDTH
    wide = HEADS_PER_STEP * WIDTH
    rows = pl.BlockSpec((length, wide), lambda h: (0, h))
    rim = pl.BlockSpec((RIM, wide), lambda h: (0, h))
    taps = pl.BlockSpec((KW, wide), lambda h: (0, h))
    return pl.pallas_call(
        local_kernel,
        grid=(heads // HEADS_PER_STEP,),
        in_specs=[rows, rows, rows, pl.BlockSpec((length, heads), lambda h: (0, 0)),
                  rim, rim, rim, taps, taps, taps],
        out_specs=[
            pl.BlockSpec((HEADS_PER_STEP, length, 2 * WIDTH), lambda h: (h, 0, 0)),
            pl.BlockSpec((HEADS_PER_STEP, WIDTH, 2 * WIDTH), lambda h: (h, 0, 0)),
        ],
        out_shape=[
            jax.ShapeDtypeStruct((heads, length, 2 * WIDTH), F32),
            jax.ShapeDtypeStruct((heads, WIDTH, 2 * WIDTH), F32),
        ],
        scratch_shapes=[pltpu.VMEM((RIM + length, WIDTH), F32)] * (3 * HEADS_PER_STEP),
        compiler_params=pltpu.CompilerParams(vmem_limit_bytes=48 * 2**20),
        name="local_pass",
    )(q, k, v, beta, *rims, conv_q, conv_k, conv_v)


def finish_kernel(part_ref, state_ref, gain_ref, out_ref):
    for i in range(part_ref.shape[0]):
        part = part_ref[i]
        o = part[:, WIDTH:] + mm_square(part[:, :WIDTH], state_ref[i])
        scale = lax.rsqrt(jnp.mean(o * o, axis=-1, keepdims=True) + 1e-05)
        out_ref[:, i * WIDTH : (i + 1) * WIDTH] = (o * scale * gain_ref[...]).astype(BF16)


def finish_pass(parts, states, gain):
    heads, length, ignored = parts.shape
    per = 2
    return pl.pallas_call(
        finish_kernel,
        grid=(heads // per,),
        in_specs=[
            pl.BlockSpec((per, length, 2 * WIDTH), lambda h: (h, 0, 0)),
            pl.BlockSpec((per, WIDTH, WIDTH), lambda h: (h, 0, 0)),
            pl.BlockSpec((1, WIDTH), lambda h: (0, 0)),
        ],
        out_specs=pl.BlockSpec((length, per * WIDTH), lambda h: (0, h)),
        out_shape=jax.ShapeDtypeStruct((length, heads * WIDTH), BF16),
        compiler_params=pltpu.CompilerParams(vmem_limit_bytes=48 * 2**20),
        name="finish_pass",
    )(parts, states, gain.reshape(1, WIDTH))


def shifted(value, axis):
    peers = lax.axis_size(axis)
    return lax.ppermute(value, axis, [(i, i + 1) for i in range(peers - 1)])


def times(a, b):
    return jnp.einsum("hij,hjv->hiv", a, b, precision=peak_level)


def incoming_states(summary):
    group = lax.axis_size("head")
    held = lax.all_to_all(summary, "head", split_axis=0, concat_axis=0, tiled=True)
    held = held.reshape(group, -1, WIDTH, 2 * WIDTH)
    before = [None, held[0]]
    for c in range(1, group):
        moved = times(held[c][:, :, :WIDTH], before[-1])
        before.append(moved.at[:, :, WIDTH:].add(held[c][:, :, WIDTH:]))
    transfer, local = before[-1][:, :, :WIDTH], before[-1][:, :, WIDTH:]
    arrived = jnp.zeros_like(local)
    for ignored in range(lax.axis_size("seq") - 1):
        arrived = shifted(times(transfer, arrived) + local, "seq")
    states = [arrived]
    for c in range(1, group):
        states.append(times(before[c][:, :, :WIDTH], arrived) + before[c][:, :, WIDTH:])
    states = jnp.concatenate(states, axis=0)
    return lax.all_to_all(states, "head", split_axis=0, concat_axis=0, tiled=True)


def shards(q_in, k_in, v_in, beta, conv_q, conv_k, conv_v, out_gain):
    edges = jnp.stack([q_in[-RIM:], k_in[-RIM:], v_in[-RIM:]])
    rims = shifted(edges, ("seq", "head"))
    parts, summary = local_pass(
        q_in, k_in, v_in, beta.astype(F32), [rims[0], rims[1], rims[2]], conv_q, conv_k, conv_v
    )
    return finish_pass(parts, incoming_states(summary), out_gain)


def solution(mesh):
    rows = P(("seq", "head"), None)
    in_specs = (rows, rows, rows, rows, P(), P(), P(), P())
    return jax.shard_map(
        shards, mesh=mesh, in_specs=in_specs, out_specs=rows, check_vma=False
    )
```

```python
import jax
import jax.numpy as jnp
from jax import lax
from jax.experimental import pallas as pl
from jax.experimental.pallas import tpu as pltpu
from jax.sharding import PartitionSpec as P

WIDTH = 128
CHUNK = 128
KW = 4
RIM = 16
BASE = 8
HEADS_PER_STEP = 4

F32 = jnp.float32
BF16 = jnp.bfloat16
MESH = pl.DeviceIdType.MESH


def split(x):
    hi = x.astype(BF16)
    return hi, (x - hi.astype(F32)).astype(BF16)


def dot(a, b):
    return jnp.dot(a, b, preferred_element_type=F32)


def wide_left(a):
    hi, lo = split(a)
    return jnp.concatenate([hi, lo], axis=1)


def square_right(b):
    row = jnp.concatenate(split(b), axis=1)
    return jnp.concatenate([row, row], axis=0)


def fold(x):
    return x[:, :WIDTH] + x[:, WIDTH:]


def mm_square(a, b):
    return fold(dot(wide_left(a), square_right(b)))


def mm_wide(a, b):
    hi, lo = split(b)
    left = wide_left(a)
    return dot(left, jnp.concatenate([hi, hi], axis=0)) + dot(left[:, : a.shape[1]], lo)


def gram(rows, keys):
    hi, lo = split(keys)
    right = jnp.concatenate(
        [jnp.concatenate([hi, hi], axis=1), jnp.concatenate([lo, lo], axis=1)], axis=0
    )
    out = lax.dot_general(
        wide_left(rows), right, (((1,), (1,)), ((), ())), preferred_element_type=F32
    )
    return fold(out)


def base_inverse(g):
    lane = lax.broadcasted_iota(jnp.int32, (BASE, CHUNK), 1)
    sub = lax.broadcasted_iota(jnp.int32, (BASE, CHUNK), 0)
    groups = CHUNK // BASE
    packed = jnp.zeros((BASE, CHUNK), F32)
    for i in range(groups):
        packed = jnp.where(lane // BASE == i, g[i * BASE : (i + 1) * BASE, :], packed)
    x = jnp.where(lane % BASE == sub, 1.0, 0.0).astype(F32)
    for j in range(BASE - 1):
        column = jnp.where(lane % BASE == j, packed, 0.0)
        if j:
            column = pltpu.roll(column, CHUNK - j, 1)
        for by in (1, 2, 4):
            column = column + pltpu.roll(column, by, 1)
        x = x - column * jnp.broadcast_to(x[j : j + 1, :], (BASE, CHUNK))
    return jnp.concatenate(
        [jnp.where(lane // BASE == i, x, 0.0) for i in range(groups)], axis=0
    )


def lower_inverses(gs):
    invs = [base_inverse(g) for g in gs]
    col = lax.broadcasted_iota(jnp.int32, (CHUNK, CHUNK), 1)
    row = lax.broadcasted_iota(jnp.int32, (CHUNK, CHUNK), 0)
    size = BASE
    while size < CHUNK:
        pairs = CHUNK // (2 * size)
        low = [slice((2 * p + 1) * size, (2 * p + 2) * size) for p in range(pairs)]
        up = [slice(2 * p * size, (2 * p + 1) * size) for p in range(pairs)]
        corner_mask = col // size == row // size - 1
        zero = jnp.zeros((size, CHUNK), F32)
        olds, products = [], []
        for g, inv in zip(gs, invs):
            corner = jnp.where(corner_mask, g, 0.0)
            corner = jnp.concatenate([corner[s] for s in low], axis=0)
            olds.append(jnp.concatenate([inv[s] for s in low], axis=0))
            products.append(mm_square(corner, inv))
        fulls = [
            jnp.concatenate(
                [t for p in range(pairs) for t in (zero, e[p * size : (p + 1) * size])], axis=0
            )
            for e in products
        ]
        news = [old - mm_square(old, full) for old, full in zip(olds, fulls)]
        invs = [
            jnp.concatenate(
                [t for p in range(pairs) for t in (inv[up[p]], new[p * size : (p + 1) * size])],
                axis=0,
            )
            for inv, new in zip(invs, news)
        ]
        size *= 2
    return invs


def conv_silu(x_ref, rim_ref, w_ref, pad, lanes):
    length = x_ref.shape[0]
    pad[0:RIM, :] = rim_ref[:, lanes].astype(F32)
    pad[RIM : RIM + length, :] = x_ref[:, lanes].astype(F32)
    w = w_ref[:, lanes]
    first = RIM - (KW - 1)
    summed = w[0:1, :] * pad[first : first + length, :]
    for j in range(1, KW):
        summed = summed + w[j : j + 1, :] * pad[first + j : first + j + length, :]
    return summed / (1.0 + jnp.exp(-summed))


def unit_rows(x):
    return x * lax.rsqrt(jnp.sum(x * x, axis=-1, keepdims=True) + 1e-06)


def local_kernel(q_ref, k_ref, v_ref, b_ref, qr_ref, kr_ref, vr_ref, cq_ref, ck_ref, cv_ref,
                 out_ref, sum_ref, *pads):
    length = q_ref.shape[0]
    step = pl.program_id(0)
    chunks = length // CHUNK
    row = lax.broadcasted_iota(jnp.int32, (CHUNK, CHUNK), 0)
    col = lax.broadcasted_iota(jnp.int32, (CHUNK, CHUNK), 1)
    beta = b_ref[...]
    which = lax.broadcasted_iota(jnp.int32, beta.shape, 1)
    chunk_rows, grams, scores = [], [], []
    for i in range(HEADS_PER_STEP):
        lanes = slice(i * WIDTH, (i + 1) * WIDTH)
        q = unit_rows(conv_silu(q_ref, qr_ref, cq_ref, pads[3 * i], lanes))
        k = unit_rows(conv_silu(k_ref, kr_ref, ck_ref, pads[3 * i + 1], lanes))
        v = conv_silu(v_ref, vr_ref, cv_ref, pads[3 * i + 2], lanes)
        head = step * HEADS_PER_STEP + i
        b = jnp.sum(jnp.where(which == head, beta, 0.0), axis=1, keepdims=True)
        for n in range(chunks):
            rows = slice(n * CHUNK, (n + 1) * CHUNK)
            qn, kn, vn, bn = q[rows], k[rows], v[rows], b[rows]
            both = gram(jnp.concatenate([qn, kn], axis=0), kn)
            p = jnp.where(row >= col, both[:CHUNK], 0.0)
            grams.append(jnp.where(row > col, both[CHUNK:] * bn, 0.0))
            scores.append(jnp.concatenate([p, kn.T], axis=0))
            chunk_rows.append((qn, jnp.concatenate([kn * bn, vn * bn], axis=1)))
    prepared = [
        (qn, pk, mm_wide(inv, kv))
        for (qn, kv), pk, inv in zip(chunk_rows, scores, lower_inverses(grams))
    ]
    zero = jnp.zeros((CHUNK, WIDTH), F32)
    for n in range(chunks):
        now = [prepared[i * chunks + n] for i in range(HEADS_PER_STEP)]
        if n == 0:
            eye = jnp.where(row == col, 1.0, 0.0).astype(F32)
            states = [jnp.concatenate([eye, zero], axis=1)] * HEADS_PER_STEP
            fresh = [
                jnp.concatenate([-wu[:, :WIDTH], wu[:, WIDTH:]], axis=1) for ignored, pk, wu in now
            ]
            seen = [jnp.concatenate([qn, zero], axis=1) for qn, pk, wu in now]
        else:
            moved = [
                mm_wide(jnp.concatenate([wu[:, :WIDTH], qn], axis=0), state)
                for (qn, pk, wu), state in zip(now, states)
            ]
            fresh = [
                jnp.concatenate([zero, wu[:, WIDTH:]], axis=1) - m[:CHUNK]
                for (qn, pk, wu), m in zip(now, moved)
            ]
            seen = [m[CHUNK:] for m in moved]
        added = [mm_wide(pk, f) for (qn, pk, wu), f in zip(now, fresh)]
        for i in range(HEADS_PER_STEP):
            out_ref[i, n * CHUNK : (n + 1) * CHUNK, :] = seen[i] + added[i][:CHUNK]
        states = [state + a[CHUNK:] for state, a in zip(states, added)]
    for i in range(HEADS_PER_STEP):
        sum_ref[i, :, :] = states[i]


def local_pass(q, k, v, beta, rims, conv_q, conv_k, conv_v):
    length, total = q.shape
    heads = total // WIDTH
    wide = HEADS_PER_STEP * WIDTH
    rows = pl.BlockSpec((length, wide), lambda h: (0, h))
    rim = pl.BlockSpec((RIM, wide), lambda h: (0, h))
    taps = pl.BlockSpec((KW, wide), lambda h: (0, h))
    return pl.pallas_call(
        local_kernel,
        grid=(heads // HEADS_PER_STEP,),
        in_specs=[rows, rows, rows, pl.BlockSpec((length, heads), lambda h: (0, 0)),
                  rim, rim, rim, taps, taps, taps],
        out_specs=[
            pl.BlockSpec((HEADS_PER_STEP, length, 2 * WIDTH), lambda h: (h, 0, 0)),
            pl.BlockSpec((HEADS_PER_STEP, WIDTH, 2 * WIDTH), lambda h: (h, 0, 0)),
        ],
        out_shape=[
            jax.ShapeDtypeStruct((heads, length, 2 * WIDTH), F32),
            jax.ShapeDtypeStruct((heads, WIDTH, 2 * WIDTH), F32),
        ],
        scratch_shapes=[pltpu.VMEM((RIM + length, WIDTH), F32)] * (3 * HEADS_PER_STEP),
        compiler_params=pltpu.CompilerParams(vmem_limit_bytes=48 * 2**20),
        name="local_pass",
    )(q, k, v, beta, *rims, conv_q, conv_k, conv_v)


def finish_kernel(part_ref, state_ref, gain_ref, out_ref):
    for i in range(part_ref.shape[0]):
        part = part_ref[i]
        o = part[:, WIDTH:] + mm_square(part[:, :WIDTH], state_ref[i])
        scale = lax.rsqrt(jnp.mean(o * o, axis=-1, keepdims=True) + 1e-05)
        out_ref[:, i * WIDTH : (i + 1) * WIDTH] = (o * scale * gain_ref[...]).astype(BF16)


def finish_pass(parts, states, gain):
    heads, length, ignored = parts.shape
    per = 2
    return pl.pallas_call(
        finish_kernel,
        grid=(heads // per,),
        in_specs=[
            pl.BlockSpec((per, length, 2 * WIDTH), lambda h: (h, 0, 0)),
            pl.BlockSpec((per, WIDTH, WIDTH), lambda h: (h, 0, 0)),
            pl.BlockSpec((1, WIDTH), lambda h: (0, 0)),
        ],
        out_specs=pl.BlockSpec((length, per * WIDTH), lambda h: (0, h)),
        out_shape=jax.ShapeDtypeStruct((length, heads * WIDTH), BF16),
        compiler_params=pltpu.CompilerParams(vmem_limit_bytes=48 * 2**20),
        name="finish_pass",
    )(parts, states, gain.reshape(1, WIDTH))


def shifted(value, axis):
    peers = lax.axis_size(axis)
    return lax.ppermute(value, axis, [(i, i + 1) for i in range(peers - 1)])


def exchange_kernel(sum_ref, state_ref, held, pre, chained, leaving, outgoing,
                    give_send, give_recv, chain_send, chain_recv, back_send, back_recv):
    group, local = held.shape[0], held.shape[1]
    me, place = lax.axis_index("head"), lax.axis_index("seq")
    length = lax.axis_size("seq")
    peers = [lax.rem(me + d, group) for d in range(group)]
    later, earlier = lax.rem(place + 1, length), lax.rem(place + length - 1, length)

    barrier = pltpu.get_barrier_semaphore()
    for peer in peers[1:]:
        pl.semaphore_signal(barrier, inc=1, device_id={"head": peer}, device_id_type=MESH)
    for side in (later, earlier):
        pl.semaphore_signal(barrier, inc=1, device_id={"seq": side}, device_id_type=MESH)
    pl.semaphore_wait(barrier, group + 1)

    def give(d, j):
        return pltpu.make_async_remote_copy(
            src_ref=sum_ref.at[peers[d] * local + j],
            dst_ref=held.at[me, j],
            send_sem=give_send.at[d - 1, j],
            recv_sem=give_recv.at[d - 1, j],
            device_id={"head": peers[d]},
            device_id_type=MESH,
        )

    def back(d, j):
        return pltpu.make_async_remote_copy(
            src_ref=outgoing.at[peers[d], j],
            dst_ref=state_ref.at[me * local + j],
            send_sem=back_send.at[d - 1, j],
            recv_sem=back_recv.at[d - 1, j],
            device_id={"head": peers[d]},
            device_id_type=MESH,
        )

    def chain(j):
        return pltpu.make_async_remote_copy(
            src_ref=leaving.at[j],
            dst_ref=chained.at[j],
            send_sem=chain_send.at[j],
            recv_sem=chain_recv.at[j],
            device_id={"seq": later},
            device_id_type=MESH,
        )

    @pl.loop(0, local)
    def _(j):
        for d in range(1, group):
            give(d, j).start()

    @pl.loop(0, local)
    def _(j):
        held[me, j] = sum_ref[me * local + j]
        for d in range(1, group):
            give(d, j).wait_recv()
        total = held[0, j]
        for c in range(1, group):
            pre[c] = total
            step = held[c, j]
            total = mm_wide(step[:, :WIDTH], total)
            total = jnp.concatenate(
                [total[:, :WIDTH], total[:, WIDTH:] + step[:, WIDTH:]], axis=1
            )

        @pl.when(place == 0)
        def _():
            chained[j] = jnp.zeros((WIDTH, WIDTH), F32)

        @pl.when(place > 0)
        def _():
            chain(j).wait_recv()

        arrived = chained[j]
        leaving[j] = mm_square(total[:, :WIDTH], arrived) + total[:, WIDTH:]

        @pl.when(place < length - 1)
        def _():
            chain(j).start()

        outgoing[0, j] = arrived
        for c in range(1, group):
            before = pre[c]
            outgoing[c, j] = mm_square(before[:, :WIDTH], arrived) + before[:, WIDTH:]
        for d in range(1, group):
            back(d, j).start()
        state_ref[me * local + j] = outgoing[me, j]

    @pl.loop(0, local)
    def _(j):
        for d in range(1, group):
            give(d, j).wait_send()
            back(d, j).wait()

        @pl.when(place < length - 1)
        def _():
            chain(j).wait_send()


def incoming_states(summary):
    group = lax.axis_size("head")
    heads = summary.shape[0]
    local = heads // group
    square = (WIDTH, WIDTH)
    pairs = pltpu.SemaphoreType.DMA((group - 1, local))
    singles = pltpu.SemaphoreType.DMA((local,))
    return pl.pallas_call(
        exchange_kernel,
        in_specs=[pl.BlockSpec(memory_space=pltpu.VMEM)],
        out_specs=pl.BlockSpec(memory_space=pltpu.VMEM),
        out_shape=jax.ShapeDtypeStruct((heads,) + square, F32),
        scratch_shapes=[
            pltpu.VMEM((group, local, WIDTH, 2 * WIDTH), F32),
            pltpu.VMEM((group, WIDTH, 2 * WIDTH), F32),
            pltpu.VMEM((local,) + square, F32),
            pltpu.VMEM((local,) + square, F32),
            pltpu.VMEM((group, local) + square, F32),
            pairs, pairs, singles, singles, pairs, pairs,
        ],
        compiler_params=pltpu.CompilerParams(
            collective_id=0, has_side_effects=True, vmem_limit_bytes=32 * 2**20
        ),
        name="exchange",
    )(summary)


def shards(q_in, k_in, v_in, beta, conv_q, conv_k, conv_v, out_gain):
    edges = jnp.stack([q_in[-RIM:], k_in[-RIM:], v_in[-RIM:]])
    rims = shifted(edges, ("seq", "head"))
    parts, summary = local_pass(
        q_in, k_in, v_in, beta.astype(F32), [rims[0], rims[1], rims[2]], conv_q, conv_k, conv_v
    )
    return finish_pass(parts, incoming_states(summary), out_gain)


def solution(mesh):
    rows = P(("seq", "head"), None)
    in_specs = (rows, rows, rows, rows, P(), P(), P(), P())
    return jax.shard_map(
        shards, mesh=mesh, in_specs=in_specs, out_specs=rows, check_vma=False
    )
```

```python
import jax
import jax.numpy as jnp
from jax import lax
from jax.experimental import pallas as pl
from jax.experimental.pallas import tpu as pltpu
from jax.sharding import PartitionSpec as P

WIDTH = 128
CHUNK = 128
KW = 4
RIM = 16
BASE = 8
HEADS_PER_STEP = 4

F32 = jnp.float32
BF16 = jnp.bfloat16
MESH = pl.DeviceIdType.MESH


def split(x):
    hi = x.astype(BF16)
    return hi, (x - hi.astype(F32)).astype(BF16)


def dot(a, b):
    return jnp.dot(a, b, preferred_element_type=F32)


def wide_left(a):
    hi, lo = split(a)
    return jnp.concatenate([hi, lo], axis=1)


def square_right(b):
    row = jnp.concatenate(split(b), axis=1)
    return jnp.concatenate([row, row], axis=0)


def fold(x):
    return x[:, :WIDTH] + x[:, WIDTH:]


def mm_square(a, b):
    return fold(dot(wide_left(a), square_right(b)))


def mm_wide(a, b):
    hi, lo = split(b)
    left = wide_left(a)
    return dot(left, jnp.concatenate([hi, hi], axis=0)) + dot(left[:, : a.shape[1]], lo)


def gram(rows, keys):
    hi, lo = split(keys)
    right = jnp.concatenate(
        [jnp.concatenate([hi, hi], axis=1), jnp.concatenate([lo, lo], axis=1)], axis=0
    )
    out = lax.dot_general(
        wide_left(rows), right, (((1,), (1,)), ((), ())), preferred_element_type=F32
    )
    return fold(out)


def base_inverse(g):
    lane = lax.broadcasted_iota(jnp.int32, (BASE, CHUNK), 1)
    sub = lax.broadcasted_iota(jnp.int32, (BASE, CHUNK), 0)
    groups = CHUNK // BASE
    packed = jnp.zeros((BASE, CHUNK), F32)
    for i in range(groups):
        packed = jnp.where(lane // BASE == i, g[i * BASE : (i + 1) * BASE, :], packed)
    x = jnp.where(lane % BASE == sub, 1.0, 0.0).astype(F32)
    for j in range(BASE - 1):
        column = jnp.where(lane % BASE == j, packed, 0.0)
        if j:
            column = pltpu.roll(column, CHUNK - j, 1)
        for by in (1, 2, 4):
            column = column + pltpu.roll(column, by, 1)
        x = x - column * jnp.broadcast_to(x[j : j + 1, :], (BASE, CHUNK))
    return jnp.concatenate(
        [jnp.where(lane // BASE == i, x, 0.0) for i in range(groups)], axis=0
    )


def lower_inverses(gs):
    invs = [base_inverse(g) for g in gs]
    col = lax.broadcasted_iota(jnp.int32, (CHUNK, CHUNK), 1)
    row = lax.broadcasted_iota(jnp.int32, (CHUNK, CHUNK), 0)
    size = BASE
    while size < CHUNK:
        pairs = CHUNK // (2 * size)
        low = [slice((2 * p + 1) * size, (2 * p + 2) * size) for p in range(pairs)]
        up = [slice(2 * p * size, (2 * p + 1) * size) for p in range(pairs)]
        corner_mask = col // size == row // size - 1
        zero = jnp.zeros((size, CHUNK), F32)
        olds, products = [], []
        for g, inv in zip(gs, invs):
            corner = jnp.where(corner_mask, g, 0.0)
            corner = jnp.concatenate([corner[s] for s in low], axis=0)
            olds.append(jnp.concatenate([inv[s] for s in low], axis=0))
            products.append(mm_square(corner, inv))
        fulls = [
            jnp.concatenate(
                [t for p in range(pairs) for t in (zero, e[p * size : (p + 1) * size])], axis=0
            )
            for e in products
        ]
        news = [old - mm_square(old, full) for old, full in zip(olds, fulls)]
        invs = [
            jnp.concatenate(
                [t for p in range(pairs) for t in (inv[up[p]], new[p * size : (p + 1) * size])],
                axis=0,
            )
            for inv, new in zip(invs, news)
        ]
        size *= 2
    return invs


def conv_silu(x_ref, rim_ref, w_ref, pad, lanes):
    length = x_ref.shape[0]
    pad[0:RIM, :] = rim_ref[:, lanes].astype(F32)
    pad[RIM : RIM + length, :] = x_ref[:, lanes].astype(F32)
    w = w_ref[:, lanes]
    first = RIM - (KW - 1)
    summed = w[0:1, :] * pad[first : first + length, :]
    for j in range(1, KW):
        summed = summed + w[j : j + 1, :] * pad[first + j : first + j + length, :]
    return summed / (1.0 + jnp.exp(-summed))


def unit_rows(x):
    return x * lax.rsqrt(jnp.sum(x * x, axis=-1, keepdims=True) + 1e-06)


def local_kernel(q_ref, k_ref, v_ref, b_ref, qr_ref, kr_ref, vr_ref, cq_ref, ck_ref, cv_ref,
                 out_ref, sum_ref, *pads):
    length = q_ref.shape[0]
    step = pl.program_id(0)
    chunks = length // CHUNK
    row = lax.broadcasted_iota(jnp.int32, (CHUNK, CHUNK), 0)
    col = lax.broadcasted_iota(jnp.int32, (CHUNK, CHUNK), 1)
    beta = b_ref[...]
    which = lax.broadcasted_iota(jnp.int32, beta.shape, 1)
    chunk_rows, grams, scores = [], [], []
    for i in range(HEADS_PER_STEP):
        lanes = slice(i * WIDTH, (i + 1) * WIDTH)
        q = unit_rows(conv_silu(q_ref, qr_ref, cq_ref, pads[3 * i], lanes))
        k = unit_rows(conv_silu(k_ref, kr_ref, ck_ref, pads[3 * i + 1], lanes))
        v = conv_silu(v_ref, vr_ref, cv_ref, pads[3 * i + 2], lanes)
        head = step * HEADS_PER_STEP + i
        b = jnp.sum(jnp.where(which == head, beta, 0.0), axis=1, keepdims=True)
        for n in range(chunks):
            rows = slice(n * CHUNK, (n + 1) * CHUNK)
            qn, kn, vn, bn = q[rows], k[rows], v[rows], b[rows]
            both = gram(jnp.concatenate([qn, kn], axis=0), kn)
            p = jnp.where(row >= col, both[:CHUNK], 0.0)
            grams.append(jnp.where(row > col, both[CHUNK:] * bn, 0.0))
            scores.append(jnp.concatenate([p, kn.T], axis=0))
            chunk_rows.append((qn, jnp.concatenate([kn * bn, vn * bn], axis=1)))
    prepared = [
        (qn, pk, mm_wide(inv, kv))
        for (qn, kv), pk, inv in zip(chunk_rows, scores, lower_inverses(grams))
    ]
    zero = jnp.zeros((CHUNK, WIDTH), F32)
    for n in range(chunks):
        now = [prepared[i * chunks + n] for i in range(HEADS_PER_STEP)]
        if n == 0:
            eye = jnp.where(row == col, 1.0, 0.0).astype(F32)
            states = [jnp.concatenate([eye, zero], axis=1)] * HEADS_PER_STEP
            fresh = [
                jnp.concatenate([-wu[:, :WIDTH], wu[:, WIDTH:]], axis=1) for ignored, pk, wu in now
            ]
            seen = [jnp.concatenate([qn, zero], axis=1) for qn, pk, wu in now]
        else:
            moved = [
                mm_wide(jnp.concatenate([wu[:, :WIDTH], qn], axis=0), state)
                for (qn, pk, wu), state in zip(now, states)
            ]
            fresh = [
                jnp.concatenate([zero, wu[:, WIDTH:]], axis=1) - m[:CHUNK]
                for (qn, pk, wu), m in zip(now, moved)
            ]
            seen = [m[CHUNK:] for m in moved]
        added = [mm_wide(pk, f) for (qn, pk, wu), f in zip(now, fresh)]
        for i in range(HEADS_PER_STEP):
            out_ref[i, n * CHUNK : (n + 1) * CHUNK, :] = seen[i] + added[i][:CHUNK]
        states = [state + a[CHUNK:] for state, a in zip(states, added)]
    for i in range(HEADS_PER_STEP):
        sum_ref[i, :, :] = states[i]


def local_pass(q, k, v, beta, rims, conv_q, conv_k, conv_v):
    length, total = q.shape
    heads = total // WIDTH
    wide = HEADS_PER_STEP * WIDTH
    rows = pl.BlockSpec((length, wide), lambda h: (0, h))
    rim = pl.BlockSpec((RIM, wide), lambda h: (0, h))
    taps = pl.BlockSpec((KW, wide), lambda h: (0, h))
    return pl.pallas_call(
        local_kernel,
        grid=(heads // HEADS_PER_STEP,),
        in_specs=[rows, rows, rows, pl.BlockSpec((length, heads), lambda h: (0, 0)),
                  rim, rim, rim, taps, taps, taps],
        out_specs=[
            pl.BlockSpec((HEADS_PER_STEP, length, 2 * WIDTH), lambda h: (h, 0, 0)),
            pl.BlockSpec((HEADS_PER_STEP, WIDTH, 2 * WIDTH), lambda h: (h, 0, 0)),
        ],
        out_shape=[
            jax.ShapeDtypeStruct((heads, length, 2 * WIDTH), F32),
            jax.ShapeDtypeStruct((heads, WIDTH, 2 * WIDTH), F32),
        ],
        scratch_shapes=[pltpu.VMEM((RIM + length, WIDTH), F32)] * (3 * HEADS_PER_STEP),
        compiler_params=pltpu.CompilerParams(vmem_limit_bytes=60 * 2**20),
        name="local_pass",
    )(q, k, v, beta, *rims, conv_q, conv_k, conv_v)


def finish_kernel(part_ref, state_ref, gain_ref, out_ref):
    for i in range(part_ref.shape[0]):
        part = part_ref[i]
        o = part[:, WIDTH:] + mm_square(part[:, :WIDTH], state_ref[i])
        scale = lax.rsqrt(jnp.mean(o * o, axis=-1, keepdims=True) + 1e-05)
        out_ref[:, i * WIDTH : (i + 1) * WIDTH] = (o * scale * gain_ref[...]).astype(BF16)


def finish_pass(parts, states, gain):
    heads, length, ignored = parts.shape
    per = 4
    return pl.pallas_call(
        finish_kernel,
        grid=(heads // per,),
        in_specs=[
            pl.BlockSpec((per, length, 2 * WIDTH), lambda h: (h, 0, 0)),
            pl.BlockSpec((per, WIDTH, WIDTH), lambda h: (h, 0, 0)),
            pl.BlockSpec((1, WIDTH), lambda h: (0, 0)),
        ],
        out_specs=pl.BlockSpec((length, per * WIDTH), lambda h: (0, h)),
        out_shape=jax.ShapeDtypeStruct((length, heads * WIDTH), BF16),
        compiler_params=pltpu.CompilerParams(vmem_limit_bytes=24 * 2**20),
        name="finish_pass",
    )(parts, states, gain.reshape(1, WIDTH))


def shifted(value, axis):
    peers = lax.axis_size(axis)
    return lax.ppermute(value, axis, [(i, i + 1) for i in range(peers - 1)])


def exchange_kernel(sum_ref, state_ref, held, pre, chained, leaving, outgoing,
                    give_send, give_recv, chain_send, chain_recv, back_send, back_recv):
    group, local = held.shape[0], held.shape[1]
    me, place = lax.axis_index("head"), lax.axis_index("seq")
    length = lax.axis_size("seq")
    peers = [lax.rem(me + d, group) for d in range(group)]
    later, earlier = lax.rem(place + 1, length), lax.rem(place + length - 1, length)

    barrier = pltpu.get_barrier_semaphore()
    for peer in peers[1:]:
        pl.semaphore_signal(barrier, inc=1, device_id={"head": peer}, device_id_type=MESH)
    for side in (later, earlier):
        pl.semaphore_signal(barrier, inc=1, device_id={"seq": side}, device_id_type=MESH)
    pl.semaphore_wait(barrier, group + 1)

    def give(d, j):
        return pltpu.make_async_remote_copy(
            src_ref=sum_ref.at[peers[d] * local + j],
            dst_ref=held.at[me, j],
            send_sem=give_send.at[d - 1, j],
            recv_sem=give_recv.at[d - 1, j],
            device_id={"head": peers[d]},
            device_id_type=MESH,
        )

    def back(d, j):
        return pltpu.make_async_remote_copy(
            src_ref=outgoing.at[peers[d], j],
            dst_ref=state_ref.at[me * local + j],
            send_sem=back_send.at[d - 1, j],
            recv_sem=back_recv.at[d - 1, j],
            device_id={"head": peers[d]},
            device_id_type=MESH,
        )

    def chain(j):
        return pltpu.make_async_remote_copy(
            src_ref=leaving.at[j],
            dst_ref=chained.at[j],
            send_sem=chain_send.at[j],
            recv_sem=chain_recv.at[j],
            device_id={"seq": later},
            device_id_type=MESH,
        )

    for d in range(1, group):
        give(d, 0).start()

    @pl.loop(0, local)
    def _(j):
        held[me, j] = sum_ref[me * local + j]
        for d in range(1, group):
            give(d, j).wait_recv()

        @pl.when(j < local - 1)
        def _():
            for d in range(1, group):
                give(d, j + 1).start()

        total = held[0, j]
        for c in range(1, group):
            pre[c] = total
            step = held[c, j]
            total = mm_wide(step[:, :WIDTH], total)
            total = jnp.concatenate(
                [total[:, :WIDTH], total[:, WIDTH:] + step[:, WIDTH:]], axis=1
            )

        @pl.when(place == 0)
        def _():
            chained[j] = jnp.zeros((WIDTH, WIDTH), F32)

        @pl.when(place > 0)
        def _():
            chain(j).wait_recv()

        arrived = chained[j]
        leaving[j] = mm_square(total[:, :WIDTH], arrived) + total[:, WIDTH:]

        @pl.when(place < length - 1)
        def _():
            chain(j).start()

        outgoing[0, j] = arrived
        for c in range(1, group):
            before = pre[c]
            outgoing[c, j] = mm_square(before[:, :WIDTH], arrived) + before[:, WIDTH:]
        for d in range(1, group):
            back(d, j).start()
        state_ref[me * local + j] = outgoing[me, j]

    @pl.loop(0, local)
    def _(j):
        for d in range(1, group):
            give(d, j).wait_send()
            back(d, j).wait()

        @pl.when(place < length - 1)
        def _():
            chain(j).wait_send()


def incoming_states(summary):
    group = lax.axis_size("head")
    heads = summary.shape[0]
    local = heads // group
    square = (WIDTH, WIDTH)
    pairs = pltpu.SemaphoreType.DMA((group - 1, local))
    singles = pltpu.SemaphoreType.DMA((local,))
    return pl.pallas_call(
        exchange_kernel,
        in_specs=[pl.BlockSpec(memory_space=pltpu.VMEM)],
        out_specs=pl.BlockSpec(memory_space=pltpu.VMEM),
        out_shape=jax.ShapeDtypeStruct((heads,) + square, F32),
        scratch_shapes=[
            pltpu.VMEM((group, local, WIDTH, 2 * WIDTH), F32),
            pltpu.VMEM((group, WIDTH, 2 * WIDTH), F32),
            pltpu.VMEM((local,) + square, F32),
            pltpu.VMEM((local,) + square, F32),
            pltpu.VMEM((group, local) + square, F32),
            pairs, pairs, singles, singles, pairs, pairs,
        ],
        compiler_params=pltpu.CompilerParams(
            collective_id=0, has_side_effects=True, vmem_limit_bytes=20 * 2**20
        ),
        name="exchange",
    )(summary)


def shards(q_in, k_in, v_in, beta, conv_q, conv_k, conv_v, out_gain):
    edges = jnp.stack([q_in[-RIM:], k_in[-RIM:], v_in[-RIM:]])
    rims = shifted(edges, ("seq", "head"))
    parts, summary = local_pass(
        q_in, k_in, v_in, beta.astype(F32), [rims[0], rims[1], rims[2]], conv_q, conv_k, conv_v
    )
    return finish_pass(parts, incoming_states(summary), out_gain)


def solution(mesh):
    rows = P(("seq", "head"), None)
    in_specs = (rows, rows, rows, rows, P(), P(), P(), P())
    return jax.shard_map(
        shards, mesh=mesh, in_specs=in_specs, out_specs=rows, check_vma=False
    )
```

```python
import jax
import jax.numpy as jnp
from jax import lax
from jax.experimental import pallas as pl
from jax.experimental.pallas import tpu as pltpu
from jax.sharding import PartitionSpec as P

WIDTH = 128
CHUNK = 128
KW = 4
RIM = 16
BASE = 8
HEADS_PER_STEP = 4

F32 = jnp.float32
BF16 = jnp.bfloat16
MESH = pl.DeviceIdType.MESH


def split(x):
    hi = x.astype(BF16)
    return hi, (x - hi.astype(F32)).astype(BF16)


def dot(a, b):
    return jnp.dot(a, b, preferred_element_type=F32)


def wide_left(a):
    hi, lo = split(a)
    return jnp.concatenate([hi, lo], axis=1)


def square_right(b):
    row = jnp.concatenate(split(b), axis=1)
    return jnp.concatenate([row, row], axis=0)


def fold(x):
    return x[:, :WIDTH] + x[:, WIDTH:]


def mm_square(a, b):
    return fold(dot(wide_left(a), square_right(b)))


def mm_wide(a, b):
    hi, lo = split(b)
    left = wide_left(a)
    return dot(left, jnp.concatenate([hi, hi], axis=0)) + dot(left[:, : a.shape[1]], lo)


def gram(rows, keys):
    hi, lo = split(keys)
    right = jnp.concatenate(
        [jnp.concatenate([hi, hi], axis=1), jnp.concatenate([lo, lo], axis=1)], axis=0
    )
    out = lax.dot_general(
        wide_left(rows), right, (((1,), (1,)), ((), ())), preferred_element_type=F32
    )
    return fold(out)


def base_inverse(g):
    lane = lax.broadcasted_iota(jnp.int32, (BASE, CHUNK), 1)
    sub = lax.broadcasted_iota(jnp.int32, (BASE, CHUNK), 0)
    groups = CHUNK // BASE
    packed = jnp.zeros((BASE, CHUNK), F32)
    for i in range(groups):
        packed = jnp.where(lane // BASE == i, g[i * BASE : (i + 1) * BASE, :], packed)
    x = jnp.where(lane % BASE == sub, 1.0, 0.0).astype(F32)
    for j in range(BASE - 1):
        column = jnp.where(lane % BASE == j, packed, 0.0)
        if j:
            column = pltpu.roll(column, CHUNK - j, 1)
        for by in (1, 2, 4):
            column = column + pltpu.roll(column, by, 1)
        x = x - column * jnp.broadcast_to(x[j : j + 1, :], (BASE, CHUNK))
    return jnp.concatenate(
        [jnp.where(lane // BASE == i, x, 0.0) for i in range(groups)], axis=0
    )


def lower_inverses(gs):
    invs = [base_inverse(g) for g in gs]
    col = lax.broadcasted_iota(jnp.int32, (CHUNK, CHUNK), 1)
    row = lax.broadcasted_iota(jnp.int32, (CHUNK, CHUNK), 0)
    size = BASE
    while size < CHUNK:
        pairs = CHUNK // (2 * size)
        low = [slice((2 * p + 1) * size, (2 * p + 2) * size) for p in range(pairs)]
        up = [slice(2 * p * size, (2 * p + 1) * size) for p in range(pairs)]
        corner_mask = col // size == row // size - 1
        zero = jnp.zeros((size, CHUNK), F32)
        olds, products = [], []
        for g, inv in zip(gs, invs):
            corner = jnp.where(corner_mask, g, 0.0)
            corner = jnp.concatenate([corner[s] for s in low], axis=0)
            olds.append(jnp.concatenate([inv[s] for s in low], axis=0))
            products.append(mm_square(corner, inv))
        fulls = [
            jnp.concatenate(
                [t for p in range(pairs) for t in (zero, e[p * size : (p + 1) * size])], axis=0
            )
            for e in products
        ]
        news = [old - mm_square(old, full) for old, full in zip(olds, fulls)]
        invs = [
            jnp.concatenate(
                [t for p in range(pairs) for t in (inv[up[p]], new[p * size : (p + 1) * size])],
                axis=0,
            )
            for inv, new in zip(invs, news)
        ]
        size *= 2
    return invs


def conv_silu(x_ref, rim_ref, w_ref, pad, lanes):
    length = x_ref.shape[0]
    pad[0:RIM, :] = rim_ref[:, lanes].astype(F32)
    pad[RIM : RIM + length, :] = x_ref[:, lanes].astype(F32)
    w = w_ref[:, lanes]
    first = RIM - (KW - 1)
    summed = w[0:1, :] * pad[first : first + length, :]
    for j in range(1, KW):
        summed = summed + w[j : j + 1, :] * pad[first + j : first + j + length, :]
    return summed / (1.0 + jnp.exp(-summed))


def unit_rows(x):
    return x * lax.rsqrt(jnp.sum(x * x, axis=-1, keepdims=True) + 1e-06)


def local_kernel(q_ref, k_ref, v_ref, b_ref, qr_ref, kr_ref, vr_ref, cq_ref, ck_ref, cv_ref,
                 out_ref, sum_ref, *pads):
    length = q_ref.shape[0]
    step = pl.program_id(0)
    chunks = length // CHUNK
    row = lax.broadcasted_iota(jnp.int32, (CHUNK, CHUNK), 0)
    col = lax.broadcasted_iota(jnp.int32, (CHUNK, CHUNK), 1)
    beta = b_ref[...]
    which = lax.broadcasted_iota(jnp.int32, beta.shape, 1)
    chunk_rows, grams, scores = [], [], []
    for i in range(HEADS_PER_STEP):
        lanes = slice(i * WIDTH, (i + 1) * WIDTH)
        q = unit_rows(conv_silu(q_ref, qr_ref, cq_ref, pads[3 * i], lanes))
        k = unit_rows(conv_silu(k_ref, kr_ref, ck_ref, pads[3 * i + 1], lanes))
        v = conv_silu(v_ref, vr_ref, cv_ref, pads[3 * i + 2], lanes)
        head = step * HEADS_PER_STEP + i
        b = jnp.sum(jnp.where(which == head, beta, 0.0), axis=1, keepdims=True)
        for n in range(chunks):
            rows = slice(n * CHUNK, (n + 1) * CHUNK)
            qn, kn, vn, bn = q[rows], k[rows], v[rows], b[rows]
            both = gram(jnp.concatenate([qn, kn], axis=0), kn)
            p = jnp.where(row >= col, both[:CHUNK], 0.0)
            grams.append(jnp.where(row > col, both[CHUNK:] * bn, 0.0))
            scores.append(jnp.concatenate([p, kn.T], axis=0))
            chunk_rows.append((qn, jnp.concatenate([kn * bn, vn * bn], axis=1)))
    prepared = [
        (qn, pk, mm_wide(inv, kv))
        for (qn, kv), pk, inv in zip(chunk_rows, scores, lower_inverses(grams))
    ]
    zero = jnp.zeros((CHUNK, WIDTH), F32)
    for n in range(chunks):
        now = [prepared[i * chunks + n] for i in range(HEADS_PER_STEP)]
        if n == 0:
            eye = jnp.where(row == col, 1.0, 0.0).astype(F32)
            states = [jnp.concatenate([eye, zero], axis=1)] * HEADS_PER_STEP
            fresh = [
                jnp.concatenate([-wu[:, :WIDTH], wu[:, WIDTH:]], axis=1) for ignored, pk, wu in now
            ]
            seen = [jnp.concatenate([qn, zero], axis=1) for qn, pk, wu in now]
        else:
            moved = [
                mm_wide(jnp.concatenate([wu[:, :WIDTH], qn], axis=0), state)
                for (qn, pk, wu), state in zip(now, states)
            ]
            fresh = [
                jnp.concatenate([zero, wu[:, WIDTH:]], axis=1) - m[:CHUNK]
                for (qn, pk, wu), m in zip(now, moved)
            ]
            seen = [m[CHUNK:] for m in moved]
        added = [mm_wide(pk, f) for (qn, pk, wu), f in zip(now, fresh)]
        for i in range(HEADS_PER_STEP):
            out_ref[i, n * CHUNK : (n + 1) * CHUNK, :] = seen[i] + added[i][:CHUNK]
        states = [state + a[CHUNK:] for state, a in zip(states, added)]
    for i in range(HEADS_PER_STEP):
        sum_ref[i, :, :] = states[i]


def local_pass(q, k, v, beta, rims, conv_q, conv_k, conv_v):
    length, total = q.shape
    heads = total // WIDTH
    wide = HEADS_PER_STEP * WIDTH
    rows = pl.BlockSpec((length, wide), lambda h: (0, h))
    rim = pl.BlockSpec((RIM, wide), lambda h: (0, h))
    taps = pl.BlockSpec((KW, wide), lambda h: (0, h))
    return pl.pallas_call(
        local_kernel,
        grid=(heads // HEADS_PER_STEP,),
        in_specs=[rows, rows, rows, pl.BlockSpec((length, heads), lambda h: (0, 0)),
                  rim, rim, rim, taps, taps, taps],
        out_specs=[
            pl.BlockSpec((HEADS_PER_STEP, length, 2 * WIDTH), lambda h: (h, 0, 0)),
            pl.BlockSpec((HEADS_PER_STEP, WIDTH, 2 * WIDTH), lambda h: (h, 0, 0)),
        ],
        out_shape=[
            jax.ShapeDtypeStruct((heads, length, 2 * WIDTH), F32),
            jax.ShapeDtypeStruct((heads, WIDTH, 2 * WIDTH), F32),
        ],
        scratch_shapes=[pltpu.VMEM((RIM + length, WIDTH), F32)] * (3 * HEADS_PER_STEP),
        compiler_params=pltpu.CompilerParams(vmem_limit_bytes=60 * 2**20),
        name="local_pass",
    )(q, k, v, beta, *rims, conv_q, conv_k, conv_v)


def finish_kernel(part_ref, state_ref, gain_ref, out_ref):
    for i in range(part_ref.shape[0]):
        part = part_ref[i]
        o = part[:, WIDTH:] + mm_square(part[:, :WIDTH], state_ref[i])
        scale = lax.rsqrt(jnp.mean(o * o, axis=-1, keepdims=True) + 1e-05)
        out_ref[:, i * WIDTH : (i + 1) * WIDTH] = (o * scale * gain_ref[...]).astype(BF16)


def finish_pass(parts, states, gain):
    heads, length, ignored = parts.shape
    per = 4
    return pl.pallas_call(
        finish_kernel,
        grid=(heads // per,),
        in_specs=[
            pl.BlockSpec((per, length, 2 * WIDTH), lambda h: (h, 0, 0)),
            pl.BlockSpec((per, WIDTH, WIDTH), lambda h: (h, 0, 0)),
            pl.BlockSpec((1, WIDTH), lambda h: (0, 0)),
        ],
        out_specs=pl.BlockSpec((length, per * WIDTH), lambda h: (0, h)),
        out_shape=jax.ShapeDtypeStruct((length, heads * WIDTH), BF16),
        compiler_params=pltpu.CompilerParams(vmem_limit_bytes=24 * 2**20),
        name="finish_pass",
    )(parts, states, gain.reshape(1, WIDTH))


def shifted(value, axis):
    peers = lax.axis_size(axis)
    return lax.ppermute(value, axis, [(i, i + 1) for i in range(peers - 1)])


def exchange_kernel(sum_ref, state_ref, held, pre, chained, leaving, outgoing,
                    give_send, give_recv, chain_send, chain_recv, back_send, back_recv):
    group, local = held.shape[0], held.shape[1]
    me, place = lax.axis_index("head"), lax.axis_index("seq")
    length = lax.axis_size("seq")
    peers = [lax.rem(me + d, group) for d in range(group)]
    later, earlier = lax.rem(place + 1, length), lax.rem(place + length - 1, length)

    barrier = pltpu.get_barrier_semaphore()
    for peer in peers[1:]:
        pl.semaphore_signal(barrier, inc=1, device_id={"head": peer}, device_id_type=MESH)
    for side in (later, earlier):
        pl.semaphore_signal(barrier, inc=1, device_id={"seq": side}, device_id_type=MESH)
    pl.semaphore_wait(barrier, group + 1)

    def give(d, j):
        return pltpu.make_async_remote_copy(
            src_ref=sum_ref.at[peers[d] * local + j],
            dst_ref=held.at[me, j],
            send_sem=give_send.at[d - 1, j],
            recv_sem=give_recv.at[d - 1, j],
            device_id={"head": peers[d]},
            device_id_type=MESH,
        )

    def back(d, j):
        return pltpu.make_async_remote_copy(
            src_ref=outgoing.at[peers[d], j],
            dst_ref=state_ref.at[me * local + j],
            send_sem=back_send.at[d - 1, j],
            recv_sem=back_recv.at[d - 1, j],
            device_id={"head": peers[d]},
            device_id_type=MESH,
        )

    def chain(j):
        return pltpu.make_async_remote_copy(
            src_ref=leaving.at[j],
            dst_ref=chained.at[j],
            send_sem=chain_send.at[j],
            recv_sem=chain_recv.at[j],
            device_id={"seq": later},
            device_id_type=MESH,
        )

    @pl.loop(0, local)
    def _(j):
        for d in range(1, group):
            give(d, j).start()

    @pl.loop(0, local)
    def _(j):
        held[me, j] = sum_ref[me * local + j]
        for d in range(1, group):
            give(d, j).wait_recv()
        total = held[0, j]
        for c in range(1, group):
            pre[c] = total
            step = held[c, j]
            total = mm_wide(step[:, :WIDTH], total)
            total = jnp.concatenate(
                [total[:, :WIDTH], total[:, WIDTH:] + step[:, WIDTH:]], axis=1
            )

        @pl.when(place == 0)
        def _():
            chained[j] = jnp.zeros((WIDTH, WIDTH), F32)

        @pl.when(place > 0)
        def _():
            chain(j).wait_recv()

        arrived = chained[j]
        leaving[j] = mm_square(total[:, :WIDTH], arrived) + total[:, WIDTH:]

        @pl.when(place < length - 1)
        def _():
            chain(j).start()

        outgoing[0, j] = arrived
        for c in range(1, group):
            before = pre[c]
            outgoing[c, j] = mm_square(before[:, :WIDTH], arrived) + before[:, WIDTH:]
        for d in range(1, group):
            back(d, j).start()
        state_ref[me * local + j] = outgoing[me, j]

    @pl.loop(0, local)
    def _(j):
        for d in range(1, group):
            give(d, j).wait_send()
            back(d, j).wait()

        @pl.when(place < length - 1)
        def _():
            chain(j).wait_send()


def incoming_states(summary):
    group = lax.axis_size("head")
    heads = summary.shape[0]
    local = heads // group
    square = (WIDTH, WIDTH)
    pairs = pltpu.SemaphoreType.DMA((group - 1, local))
    singles = pltpu.SemaphoreType.DMA((local,))
    return pl.pallas_call(
        exchange_kernel,
        in_specs=[pl.BlockSpec(memory_space=pltpu.VMEM)],
        out_specs=pl.BlockSpec(memory_space=pltpu.VMEM),
        out_shape=jax.ShapeDtypeStruct((heads,) + square, F32),
        scratch_shapes=[
            pltpu.VMEM((group, local, WIDTH, 2 * WIDTH), F32),
            pltpu.VMEM((group, WIDTH, 2 * WIDTH), F32),
            pltpu.VMEM((local,) + square, F32),
            pltpu.VMEM((local,) + square, F32),
            pltpu.VMEM((group, local) + square, F32),
            pairs, pairs, singles, singles, pairs, pairs,
        ],
        compiler_params=pltpu.CompilerParams(
            collective_id=0, has_side_effects=True, vmem_limit_bytes=20 * 2**20
        ),
        name="exchange",
    )(summary)


def shards(q_in, k_in, v_in, beta, conv_q, conv_k, conv_v, out_gain):
    edges = jnp.stack([q_in[-RIM:], k_in[-RIM:], v_in[-RIM:]])
    rims = shifted(edges, ("seq", "head"))
    parts, summary = local_pass(
        q_in, k_in, v_in, beta.astype(F32), [rims[0], rims[1], rims[2]], conv_q, conv_k, conv_v
    )
    return finish_pass(parts, incoming_states(summary), out_gain)


def solution(mesh):
    rows = P(("seq", "head"), None)
    in_specs = (rows, rows, rows, rows, P(), P(), P(), P())
    return jax.shard_map(
        shards, mesh=mesh, in_specs=in_specs, out_specs=rows, check_vma=False
    )
```
